32 devices in a mesh: lat: 8 (over z, x), lev: 4 (over y, core).
Axes of the slice: x: 2, y: 2, z: 4, core: 2. Of those that a mesh axis runs over, the one named last changes fastest.
Arguments:
- tracer_dyn: bfloat16 [64, 72, 16, 1024], P(None, 'lev', 'lat'), may hold values from 0.19921875 to 5
- courant_lat: bfloat16 [72, 16, 1024], P('lev', 'lat'), may hold values from -0.44921875 to 0.44921875
- courant_lon: bfloat16 [72, 16, 1024], P('lev', 'lat'), may hold values from -0.44921875 to 0.44921875
- conv_matrix: bfloat16 [72, 72, 16384], P(None, None, ('lat', 'lev'))
- conv_mask: int32 [16384], P(('lat', 'lev')), may hold values from 0 to 1, as said below
- column_order: int32 [16384], P(('lat', 'lev')), may hold values from 0 to 511, as said below
- rain: bfloat16 [72, 16384], P(None, ('lat', 'lev')), may hold values from 0.019897461 to 1
- scav_rate: float32 [64], replicated, may hold values from 0.05 to 2
- pair_flag: int32 [16], replicated, may hold values from 0 to 1
Outputs:
- tracer_phys: bfloat16 [64, 72, 16384], P(None, None, ('lat', 'lev'))
The draws below stay inside these ranges and needn't reach their ends.
Inputs may be any that keep to these rules, and one draw needn't show every extreme that they name: `conv_mask`: in each aligned block of 512 entries (one span) at most 256 are 1, and some block has exactly 256. `column_order`: each aligned block of 512 entries holds every number of 0 to 511 once.
All inputs are finite; a program needn't handle non-finite values.
Results may differ from the reference program's by a relative error of at most 0.005.
Values may be sent and summed in bfloat16 or wider, within the bound.
A program may use at most 128 MiB of HBM per device.

```python
import math
import jax
import jax.numpy as jnp
from jax import lax

TRACERS = 64
LEV = 72
LON = 1024
LAT_DEV = 2
NLAT = 16
COLS = 16384
LON_BLOCK = 256
COL_DEV = 512
CONV_CAP = 256
PAIRS = 16
N_LAT = 8
N_LEV = 4


def draw_conv_matrix(key, part):
    key_diag = jax.random.fold_in(key, 11)
    key_off = jax.random.fold_in(key, 12)
    diag = jax.random.uniform(key_diag, (COLS, LEV), jnp.float32, 0.5, 1.0)
    off = jax.random.normal(key_off, (COLS, LEV, LEV), jnp.float32) * 0.4 / jnp.sqrt(1.0 * LEV)
    eye = jnp.eye(LEV, dtype=jnp.float32)
    whole = off + diag[:, :, None] * eye[None]
    return jnp.transpose(whole, (1, 2, 0)).astype(jnp.bfloat16)


def draw_conv_mask(key, part):
    spans = COLS // COL_DEV
    key_count = jax.random.fold_in(key, 21)
    key_heavy = jax.random.fold_in(key, 22)
    key_perm = jax.random.fold_in(key, 23)
    raw = jax.random.randint(key_count, (spans,), 0, CONV_CAP + 1)
    counts = jnp.maximum(raw * raw // CONV_CAP, 1)
    heavy = jax.random.randint(key_heavy, (), 0, spans)
    counts = jnp.where(jnp.arange(spans) == heavy, CONV_CAP, counts)
    keys = jax.random.split(key_perm, spans)
    ranks = jax.vmap(lambda single: jax.random.permutation(single, COL_DEV))(keys)
    return (ranks < counts[:, None]).astype(jnp.int32).reshape(COLS)


def draw_column_order(key, part):
    spans = COLS // COL_DEV
    keys = jax.random.split(jax.random.fold_in(key, 31), spans)
    perms = jax.vmap(lambda single: jax.random.permutation(single, COL_DEV))(keys)
    return perms.astype(jnp.int32).reshape(COLS)


def with_ends(values, stream_key, low, high):
    longest = values.shape.index(max(values.shape))
    spots = []
    for shift in (0, 1):
        where = [jax.random.randint(jax.random.fold_in(stream_key, axis), (), 0, length) for axis, length in enumerate(values.shape)]
        where[longest] = (where[longest] + shift) % values.shape[longest]
        spots.append(tuple(where))
    return values.at[spots[0]].set(low).at[spots[1]].set(high)


def block_scale(stream_key, dims, shards, low, high):
    def one(axis_at, parts):
        heights = jax.random.uniform(jax.random.fold_in(jax.random.fold_in(stream_key, 6), axis_at), (parts,), jnp.float32, low / len(shards), high / len(shards))
        return jnp.repeat(jnp.exp(heights), dims[axis_at] // parts).reshape((-1,) + (1,) * (len(dims) - axis_at - 1))

    loudness = one(*shards[0])
    for cut in shards[1:]:
        loudness = loudness * one(*cut)
    return loudness


def setup_inputs(seed: int = 0) -> dict:
    seeds = jax.random.split(jax.random.key(seed), 10)
    return {
        "tracer_dyn": jnp.clip(jnp.exp(math.log(5.0) - 3.2227897 * jax.random.uniform(seeds[0], (TRACERS, LEV, NLAT, LON), jnp.float32) ** block_scale(seeds[0], (TRACERS, LEV, NLAT, LON), ((1, 4), (2, 8)), -0.2, 0.2)), 0.19921875, 5.0).astype(jnp.bfloat16),
        "courant_lat": jnp.clip(jax.random.uniform(seeds[1], (LEV, NLAT, LON), jnp.float32, -0.44921875, 0.44921875) * block_scale(seeds[1], (LEV, NLAT, LON), ((0, 4), (1, 8)), -0.4, 0.0), -0.44921875, 0.44921875).astype(jnp.bfloat16),
        "courant_lon": jnp.clip(jax.random.uniform(seeds[2], (LEV, NLAT, LON), jnp.float32, -0.44921875, 0.44921875) * block_scale(seeds[2], (LEV, NLAT, LON), ((0, 4), (1, 8)), -0.4, 0.0), -0.44921875, 0.44921875).astype(jnp.bfloat16),
        "conv_matrix": draw_conv_matrix(jax.random.fold_in(seeds[9], 71), 0),
        "conv_mask": draw_conv_mask(jax.random.fold_in(seeds[9], 71), 0),
        "column_order": draw_column_order(jax.random.fold_in(seeds[9], 71), 0),
        "rain": jnp.clip(jnp.exp(math.log(1.0) - 3.9171631 * jax.random.uniform(seeds[6], (LEV, COLS), jnp.float32) ** block_scale(seeds[6], (LEV, COLS), ((1, 32),), -0.2, 0.2)), 0.019897461, 1.0).astype(jnp.bfloat16),
        "scav_rate": jnp.clip(jnp.exp(jax.random.uniform(seeds[7], (TRACERS,), jnp.float32, math.log(0.05), math.log(2.0))), 0.05, 2.0),
        "pair_flag": with_ends(jax.random.randint(seeds[8], (PAIRS,), 0, 2), jax.random.fold_in(seeds[8], 1), 0, 1).astype(jnp.int32),
    }


def advect_block(center, south_side, north_side, south_face, north_face, west_face):
    east_face = jnp.roll(west_face, -1, axis=-1)
    south_flux = south_face * jnp.where(south_face > 0, south_side, center)
    north_flux = north_face * jnp.where(north_face > 0, center, north_side)
    west_flux = west_face * jnp.where(west_face > 0, jnp.roll(center, 1, axis=-1), center)
    east_flux = east_face * jnp.where(east_face > 0, center, jnp.roll(center, -1, axis=-1))
    return center - (north_flux - south_flux) - (east_flux - west_flux)


def reference(tracer_dyn, courant_lat, courant_lon, conv_matrix, conv_mask, column_order, rain, scav_rate, pair_flag):
    south_face = courant_lat.astype(jnp.float32)
    west_face = courant_lon.astype(jnp.float32)
    north_face = jnp.concatenate([south_face[:, 1:], jnp.zeros_like(south_face[:, :1])], axis=1)

    def advect_one(tracer):
        center = tracer.astype(jnp.float32)
        zero_row = jnp.zeros_like(center[:, :1])
        south_side = jnp.concatenate([zero_row, center[:, :-1]], axis=1)
        north_side = jnp.concatenate([center[:, 1:], zero_row], axis=1)
        return advect_block(center, south_side, north_side, south_face, north_face, west_face).astype(jnp.bfloat16)

    advected = lax.map(advect_one, tracer_dyn)
    blocked = advected.reshape(TRACERS, LEV, N_LAT, LAT_DEV, N_LEV, LON_BLOCK)
    physics = jnp.transpose(blocked, (0, 1, 2, 4, 3, 5)).reshape(TRACERS, LEV, COLS)
    spans = COLS // COL_DEV
    by_span = physics.reshape(TRACERS, LEV, spans, COL_DEV).transpose(2, 0, 1, 3)
    matrices = conv_matrix.reshape(LEV, LEV, spans, COL_DEV).transpose(2, 0, 1, 3)
    masks = conv_mask.reshape(spans, COL_DEV)
    orders = column_order.reshape(spans, COL_DEV)
    rains = rain.reshape(LEV, spans, COL_DEV).transpose(1, 0, 2)

    def span_physics(items):
        tracers, matrix, mask, order, wet = items
        ordered = tracers[:, :, order].astype(jnp.float32)
        moved = jnp.einsum('kec,tec->tkc', matrix.astype(jnp.float32), ordered)
        convected = jnp.where(mask[None, None, :] > 0, moved, ordered)
        washed = convected * jnp.exp(-scav_rate[:, None, None] * wet.astype(jnp.float32)[None])
        return washed.astype(jnp.bfloat16)

    result = lax.map(span_physics, (by_span, matrices, masks, orders, rains))
    grid = result.reshape(N_LAT, N_LEV, TRACERS, LEV, COL_DEV)
    partner = jnp.roll(grid, N_LAT // 2, axis=0)
    half_flags = pair_flag.reshape(N_LAT // 2, N_LEV)
    flags = jnp.concatenate([half_flags, half_flags], axis=0)
    final = jnp.where(flags[:, :, None, None, None] > 0, partner, grid)
    return final.transpose(2, 3, 0, 1, 4).reshape(TRACERS, LEV, COLS)
```

```python
import functools

import jax
import jax.numpy as jnp
from jax import lax
from jax.experimental import pallas as pl
from jax.experimental.pallas import tpu as pltpu
from jax.sharding import PartitionSpec as P

UNIT = 8
STRIP = 16
LANES = 128
GROUP = 4


def shifted(value, axis, steps):
    count = lax.axis_size(axis)
    first, last = max(0, -steps), min(count, count - steps)
    return lax.ppermute(value, axis, [(i, i + steps) for i in range(first, last)])


def swapped(value, axis, apart):
    return lax.ppermute(value, axis, [(i, i ^ apart) for i in range(lax.axis_size(axis))])


def advect_kernel(n_lev, q0_ref, q1_ref, south_ref, north_ref, cs0_ref, cs1_ref, cn_ref, cw0_ref, cw1_ref, out_ref):
    f32 = jnp.float32
    rows, lon = q0_ref.shape
    block = lon // n_lev

    def lon_change(q, cw):
        west = cw * jnp.where(cw > 0, pltpu.roll(q, 1, 1), q)
        return pltpu.roll(west, lon - 1, 1) - west

    def strip(s, carry):
        at = pl.ds(pl.multiple_of(s * STRIP, STRIP), STRIP)
        q0, q1 = q0_ref[at, :].astype(f32), q1_ref[at, :].astype(f32)
        cs0, cs1, cn = (r[at, :].astype(f32) for r in (cs0_ref, cs1_ref, cn_ref))
        low = cs0 * jnp.where(cs0 > 0, south_ref[at, :].astype(f32), q0)
        mid = cs1 * jnp.where(cs1 > 0, q0, q1)
        high = cn * jnp.where(cn > 0, q1, north_ref[at, :].astype(f32))
        new0 = q0 - (mid - low) - lon_change(q0, cw0_ref[at, :].astype(f32))
        new1 = q1 - (high - mid) - lon_change(q1, cw1_ref[at, :].astype(f32))
        new0, new1 = new0.astype(out_ref.dtype), new1.astype(out_ref.dtype)
        for j in range(n_lev):
            out_ref[j, at, :block] = new0[:, j * block:(j + 1) * block]
            out_ref[j, at, block:] = new1[:, j * block:(j + 1) * block]
        return carry

    lax.fori_loop(0, rows // STRIP, strip, 0)


def advect(n_lev, q0, q1, south, north, faces):
    rows, lon = q0.shape
    unit = faces[0].shape[0]
    row_spec = pl.BlockSpec((unit, lon), lambda i: (i, 0))
    face_spec = pl.BlockSpec((unit, lon), lambda i: (0, 0))
    return pl.pallas_call(
        functools.partial(advect_kernel, n_lev),
        grid=(rows // unit,),
        in_specs=[row_spec] * 4 + [face_spec] * 5,
        out_specs=pl.BlockSpec((n_lev, unit, 2 * lon // n_lev), lambda i: (0, i, 0)),
        out_shape=jax.ShapeDtypeStruct((n_lev, rows, 2 * lon // n_lev), q0.dtype),
        compiler_params=pltpu.CompilerParams(vmem_limit_bytes=32 * 2**20),
        cost_estimate=pl.CostEstimate(flops=60 * rows * lon, bytes_accessed=12 * rows * lon, transcendentals=0),
        name="advect",
    )(q0, q1, south, north, *faces)


def physics_kernel(arrived_ref, placing_ref, matrix_ref, rain_ref, scav_ref, out_ref, x_ref):
    f32 = jnp.float32
    n_lev, rows, _ = arrived_ref.shape
    tracers, levels, lanes = out_ref.shape
    per = levels // n_lev
    for g in range(n_lev):
        x_ref[g] = jnp.dot(arrived_ref[g], placing_ref[...], preferred_element_type=f32)
    rain = rain_ref[...].astype(f32)

    def group(i, carry):
        t0 = i * GROUP
        sums = tuple(jnp.zeros((levels, lanes), f32) for _ in range(GROUP))
        for g in range(n_lev):
            def level(e, sums):
                m = matrix_ref[g * per + e].astype(f32)
                return tuple(
                    total + m * x_ref[g, pl.ds((t0 + u) * per + e, 1), :]
                    for u, total in enumerate(sums)
                )
            sums = lax.fori_loop(0, per, level, sums, unroll=2)
        for u in range(GROUP):
            out_ref[t0 + u] = (sums[u] * jnp.exp(-scav_ref[t0 + u] * rain)).astype(out_ref.dtype)
        return carry

    lax.fori_loop(0, tracers // GROUP, group, 0)


def physics(arrived, placing, matrix, rain, scav):
    n_lev, rows, columns = arrived.shape
    levels = rain.shape[0]
    tracers = scav.shape[0]
    return pl.pallas_call(
        physics_kernel,
        grid=(columns // LANES,),
        in_specs=[
            pl.BlockSpec(arrived.shape, lambda i: (0, 0, 0)),
            pl.BlockSpec((columns, LANES), lambda i: (0, i)),
            pl.BlockSpec((levels, levels, LANES), lambda i: (0, 0, i)),
            pl.BlockSpec((levels, LANES), lambda i: (0, i)),
            pl.BlockSpec(memory_space=pltpu.SMEM),
        ],
        out_specs=pl.BlockSpec((tracers, levels, LANES), lambda i: (0, 0, i)),
        out_shape=jax.ShapeDtypeStruct((tracers, levels, columns), arrived.dtype),
        scratch_shapes=[pltpu.VMEM((n_lev, rows, LANES), jnp.float32)],
        compiler_params=pltpu.CompilerParams(vmem_limit_bytes=40 * 2**20),
        cost_estimate=pl.CostEstimate(
            flops=40 * tracers * levels * levels * columns,
            bytes_accessed=4 * tracers * levels * columns + 2 * levels * levels * columns,
            transcendentals=tracers * levels * columns),
        name="physics",
    )(arrived, placing, matrix, rain, scav)


def chunks_of(tracers):
    units = tracers // UNIT
    parts, left, size = [], units, 1
    while left:
        take = min(size, left)
        parts.append(take * UNIT)
        left -= take
        if len(parts) >= 2:
            size = 2
    return parts


def local(tracer_dyn, courant_lat, courant_lon, conv_matrix, conv_mask, column_order, rain, scav_rate, pair_flag):
    n_lat = lax.axis_size("lat")
    n_lev = lax.axis_size("lev")
    tracers, per, _, lon = tracer_dyn.shape
    levels, _, columns = conv_matrix.shape

    def tiled(face):
        return jnp.tile(face, (UNIT, 1))

    faces = (
        tiled(courant_lat[:, 0]),
        tiled(courant_lat[:, 1]),
        tiled(shifted(courant_lat[:, 0], "lat", -1)),
        tiled(courant_lon[:, 0]),
        tiled(courant_lon[:, 1]),
    )
    parts = chunks_of(tracers)
    starts = [sum(parts[:c]) for c in range(len(parts))]
    rows = []
    for start, size in zip(starts, parts):
        piece = tracer_dyn[start:start + size]
        q0 = piece[:, :, 0].reshape(size * per, lon)
        q1 = piece[:, :, 1].reshape(size * per, lon)
        rows.append((q0, q1, shifted(q1, "lat", 1), shifted(q0, "lat", -1)))

    placing = (jnp.arange(columns, dtype=jnp.int32)[:, None] == column_order[None, :]).astype(jnp.bfloat16)
    keep = jnp.eye(levels, dtype=conv_matrix.dtype)[:, :, None]
    matrix = jnp.where(conv_mask[None, None, :] > 0, jnp.transpose(conv_matrix, (1, 0, 2)), keep)

    pair = lax.axis_index("lat") % (n_lat // 2) * n_lev + lax.axis_index("lev")
    trade = pair_flag[pair] > 0
    result = jnp.zeros((tracers, levels, columns), tracer_dyn.dtype)
    for c, (start, size) in enumerate(zip(starts, parts)):
        advected = advect(n_lev, *rows[c], faces)
        arrived = lax.all_to_all(advected, "lev", split_axis=0, concat_axis=0, tiled=True)
        washed = physics(arrived, placing, matrix, rain, scav_rate[start:start + size])
        partner = swapped(washed, "lat", n_lat // 2)
        chosen = jnp.where(trade, partner, washed)
        result = lax.dynamic_update_slice(result, chosen, (start, 0, 0))
    return result


def solution(mesh):
    placed = (
        P(None, "lev", "lat", None),
        P("lev", "lat", None),
        P("lev", "lat", None),
        P(None, None, ("lat", "lev")),
        P(("lat", "lev")),
        P(("lat", "lev")),
        P(None, ("lat", "lev")),
        P(),
        P(),
    )
    return jax.shard_map(
        local, mesh=mesh, in_specs=placed, out_specs=P(None, None, ("lat", "lev")), check_vma=False
    )
```

```python
import functools

import jax
import jax.numpy as jnp
from jax import lax
from jax.experimental import pallas as pl
from jax.experimental.pallas import tpu as pltpu
from jax.sharding import PartitionSpec as P

UNIT = 8
STRIP = 16
LANES = 128
GROUP = 4


def shifted(value, axis, steps):
    count = lax.axis_size(axis)
    first, last = max(0, -steps), min(count, count - steps)
    return lax.ppermute(value, axis, [(i, i + steps) for i in range(first, last)])


def swapped(value, axis, apart):
    return lax.ppermute(value, axis, [(i, i ^ apart) for i in range(lax.axis_size(axis))])


def split_kernel(q_ref, after_ref, q0_ref, q1_ref):
    del after_ref
    rows = q0_ref.shape[0]
    row = lax.broadcasted_iota(jnp.int32, (rows, 2 * rows), 0)
    column = lax.broadcasted_iota(jnp.int32, (rows, 2 * rows), 1)
    for a, ref in enumerate((q0_ref, q1_ref)):
        pick = (column == 2 * row + a).astype(jnp.float32).astype(q_ref.dtype)
        ref[...] = jnp.dot(pick, q_ref[...], preferred_element_type=jnp.float32).astype(ref.dtype)


def split(q, unit, after):
    rows, lon = q.shape
    half = jax.ShapeDtypeStruct((rows // 2, lon), q.dtype)
    return pl.pallas_call(
        split_kernel,
        grid=(rows // 2 // unit,),
        in_specs=[pl.BlockSpec((2 * unit, lon), lambda i: (i, 0)), pl.BlockSpec(memory_space=pl.ANY)],
        out_specs=[pl.BlockSpec((unit, lon), lambda i: (i, 0))] * 2,
        out_shape=[half, half],
        compiler_params=pltpu.CompilerParams(vmem_limit_bytes=32 * 2**20),
        cost_estimate=pl.CostEstimate(flops=4 * rows * lon, bytes_accessed=4 * rows * lon, transcendentals=0),
        name="split",
    )(q, after)


def advect_kernel(n_lev, q0_ref, q1_ref, south_ref, north_ref, cs0_ref, cs1_ref, cn_ref, cw0_ref, cw1_ref, after_ref, out_ref):
    del after_ref
    f32 = jnp.float32
    rows, lon = q0_ref.shape
    block = lon // n_lev

    def lon_change(q, cw):
        west = cw * jnp.where(cw > 0, pltpu.roll(q, 1, 1), q)
        return pltpu.roll(west, lon - 1, 1) - west

    def strip(s, carry):
        at = pl.ds(pl.multiple_of(s * STRIP, STRIP), STRIP)
        q0, q1 = q0_ref[at, :].astype(f32), q1_ref[at, :].astype(f32)
        cs0, cs1, cn = (r[at, :].astype(f32) for r in (cs0_ref, cs1_ref, cn_ref))
        low = cs0 * jnp.where(cs0 > 0, south_ref[at, :].astype(f32), q0)
        mid = cs1 * jnp.where(cs1 > 0, q0, q1)
        high = cn * jnp.where(cn > 0, q1, north_ref[at, :].astype(f32))
        new0 = q0 - (mid - low) - lon_change(q0, cw0_ref[at, :].astype(f32))
        new1 = q1 - (high - mid) - lon_change(q1, cw1_ref[at, :].astype(f32))
        new0, new1 = new0.astype(out_ref.dtype), new1.astype(out_ref.dtype)
        for j in range(n_lev):
            out_ref[j, at, :block] = new0[:, j * block:(j + 1) * block]
            out_ref[j, at, block:] = new1[:, j * block:(j + 1) * block]
        return carry

    lax.fori_loop(0, rows // STRIP, strip, 0)


def advect(n_lev, q0, q1, south, north, faces, after):
    rows, lon = q0.shape
    unit = faces[0].shape[0]
    row_spec = pl.BlockSpec((unit, lon), lambda i: (i, 0))
    face_spec = pl.BlockSpec((unit, lon), lambda i: (0, 0))
    return pl.pallas_call(
        functools.partial(advect_kernel, n_lev),
        grid=(rows // unit,),
        in_specs=[row_spec] * 4 + [face_spec] * 5 + [pl.BlockSpec(memory_space=pl.ANY)],
        out_specs=pl.BlockSpec((n_lev, unit, 2 * lon // n_lev), lambda i: (0, i, 0)),
        out_shape=jax.ShapeDtypeStruct((n_lev, rows, 2 * lon // n_lev), q0.dtype),
        compiler_params=pltpu.CompilerParams(vmem_limit_bytes=32 * 2**20),
        cost_estimate=pl.CostEstimate(flops=60 * rows * lon, bytes_accessed=12 * rows * lon, transcendentals=0),
        name="advect",
    )(q0, q1, south, north, *faces, after)


def physics_kernel(arrived_ref, placing_ref, matrix_ref, rain_ref, scav_ref, out_ref, x_ref):
    f32 = jnp.float32
    n_lev, rows, _ = arrived_ref.shape
    tracers, levels, lanes = out_ref.shape
    per = levels // n_lev
    for g in range(n_lev):
        x_ref[g] = jnp.dot(arrived_ref[g], placing_ref[...], preferred_element_type=f32)
    rain = rain_ref[...].astype(f32)

    def group(i, carry):
        t0 = i * GROUP
        sums = tuple(jnp.zeros((levels, lanes), f32) for _ in range(GROUP))
        for g in range(n_lev):
            def level(e, sums):
                m = matrix_ref[g * per + e].astype(f32)
                return tuple(
                    total + m * x_ref[g, pl.ds((t0 + u) * per + e, 1), :]
                    for u, total in enumerate(sums)
                )
            sums = lax.fori_loop(0, per, level, sums, unroll=True)
        for u in range(GROUP):
            out_ref[t0 + u] = (sums[u] * jnp.exp(-scav_ref[t0 + u] * rain)).astype(out_ref.dtype)
        return carry

    lax.fori_loop(0, tracers // GROUP, group, 0)


def physics(arrived, placing, matrix, rain, scav):
    n_lev, rows, columns = arrived.shape
    levels = rain.shape[0]
    tracers = scav.shape[0]
    return pl.pallas_call(
        physics_kernel,
        grid=(columns // LANES,),
        in_specs=[
            pl.BlockSpec(arrived.shape, lambda i: (0, 0, 0)),
            pl.BlockSpec((columns, LANES), lambda i: (0, i)),
            pl.BlockSpec((levels, levels, LANES), lambda i: (0, 0, i)),
            pl.BlockSpec((levels, LANES), lambda i: (0, i)),
            pl.BlockSpec(memory_space=pltpu.SMEM),
        ],
        out_specs=pl.BlockSpec((tracers, levels, LANES), lambda i: (0, 0, i)),
        out_shape=jax.ShapeDtypeStruct((tracers, levels, columns), arrived.dtype),
        scratch_shapes=[pltpu.VMEM((n_lev, rows, LANES), jnp.float32)],
        compiler_params=pltpu.CompilerParams(vmem_limit_bytes=40 * 2**20),
        cost_estimate=pl.CostEstimate(
            flops=40 * tracers * levels * levels * columns,
            bytes_accessed=4 * tracers * levels * columns + 2 * levels * levels * columns,
            transcendentals=tracers * levels * columns),
        name="physics",
    )(arrived, placing, matrix, rain, scav)


def chunks_of(tracers):
    units = tracers // UNIT
    parts, left, size = [], units, 1
    while left:
        take = min(size, left)
        parts.append(take * UNIT)
        left -= take
        if len(parts) >= 2:
            size = 2
    return parts


def local(tracer_dyn, courant_lat, courant_lon, conv_matrix, conv_mask, column_order, rain, scav_rate, pair_flag):
    n_lat = lax.axis_size("lat")
    n_lev = lax.axis_size("lev")
    tracers, per, _, lon = tracer_dyn.shape
    levels, _, columns = conv_matrix.shape

    def tiled(face):
        return jnp.tile(face, (UNIT, 1))

    faces = (
        tiled(courant_lat[:, 0]),
        tiled(courant_lat[:, 1]),
        tiled(shifted(courant_lat[:, 0], "lat", -1)),
        tiled(courant_lon[:, 0]),
        tiled(courant_lon[:, 1]),
    )
    parts = chunks_of(tracers)
    starts = [sum(parts[:c]) for c in range(len(parts))]
    placing = (jnp.arange(columns, dtype=jnp.int32)[:, None] == column_order[None, :]).astype(jnp.bfloat16)
    keep = jnp.eye(levels, dtype=conv_matrix.dtype)[:, :, None]
    matrix = jnp.where(conv_mask[None, None, :] > 0, jnp.transpose(conv_matrix, (1, 0, 2)), keep)

    pair = lax.axis_index("lat") % (n_lat // 2) * n_lev + lax.axis_index("lev")
    trade = pair_flag[pair] > 0
    result = jnp.zeros((tracers, levels, columns), tracer_dyn.dtype)
    def sent(c, after):
        piece = tracer_dyn[starts[c]:starts[c] + parts[c]].reshape(2 * parts[c] * per, lon)
        q0, q1 = split(piece, UNIT * per, after)
        return q0, q1, shifted(q1, "lat", 1), shifted(q0, "lat", -1)

    ahead = [sent(0, faces[0]), sent(1, faces[1])]
    washed = placing
    for c, (start, size) in enumerate(zip(starts, parts)):
        advected = advect(n_lev, *ahead[c], faces, washed)
        if c + 2 < len(parts):
            ahead.append(sent(c + 2, advected))
        arrived = lax.all_to_all(advected, "lev", split_axis=0, concat_axis=0, tiled=True)
        washed = physics(arrived, placing, matrix, rain, scav_rate[start:start + size])
        partner = swapped(washed, "lat", n_lat // 2)
        chosen = jnp.where(trade, partner, washed)
        result = lax.dynamic_update_slice(result, chosen, (start, 0, 0))
    return result


def solution(mesh):
    placed = (
        P(None, "lev", "lat", None),
        P("lev", "lat", None),
        P("lev", "lat", None),
        P(None, None, ("lat", "lev")),
        P(("lat", "lev")),
        P(("lat", "lev")),
        P(None, ("lat", "lev")),
        P(),
        P(),
    )
    return jax.shard_map(
        local, mesh=mesh, in_specs=placed, out_specs=P(None, None, ("lat", "lev")), check_vma=False
    )
```

```python
import functools

import jax
import jax.numpy as jnp
from jax import lax
from jax.experimental import pallas as pl
from jax.experimental.pallas import tpu as pltpu
from jax.sharding import PartitionSpec as P

UNIT = 8
STRIP = 16
LANES = 128
GROUP = 4
MESH = pl.DeviceIdType.MESH


def kernel(
    n_lat, n_lev, scav_ref, tracer_ref, faces_ref, placing_ref, matrix_ref, rain_ref,
    washed_ref, partner_ref,
    row0, row1, south, north, above, advected, arrived, x_ref,
    up_send, up_recv, down_send, down_recv, face_send, face_recv,
    lev_send, lev_recv, own_sem, trade_send, trade_recv,
):
    f32 = jnp.float32
    chunks, unit, lon = row0.shape
    tracers, levels, columns = washed_ref.shape
    block = lon // n_lev
    per = levels // n_lev
    lat, lev = lax.axis_index("lat"), lax.axis_index("lev")
    has_south, has_north = lat > 0, lat < n_lat - 1
    across = lax.rem(lat + n_lat // 2, n_lat)

    def remote(src, dst, send, recv, device):
        return pltpu.make_async_remote_copy(
            src_ref=src, dst_ref=dst, send_sem=send, recv_sem=recv,
            device_id=device, device_id_type=MESH)

    def up(c):
        return remote(row1.at[c], south.at[c], up_send.at[c], up_recv.at[c], (lat + 1, lev))

    def down(c):
        return remote(row0.at[c], north.at[c], down_send.at[c], down_recv.at[c], (lat - 1, lev))

    face = remote(faces_ref.at[0], above, face_send, face_recv, (lat - 1, lev))

    def exchange(c, s):
        to = lax.rem(lev + s, n_lev)
        return remote(advected.at[c, to], arrived.at[c, lev],
                      lev_send.at[c, s], lev_recv.at[c, s], (lat, to))

    def exchanged(c, s):
        source = lax.rem(lev + n_lev - s, n_lev)
        return remote(advected.at[c, source], arrived.at[c, source],
                      lev_send.at[c, s], lev_recv.at[c, s], (lat, source))

    def own(c):
        return pltpu.make_async_copy(advected.at[c, lev], arrived.at[c, lev], own_sem.at[c])

    def trade(c):
        part = pl.ds(c * UNIT, UNIT)
        return remote(washed_ref.at[part], partner_ref.at[part],
                      trade_send.at[c], trade_recv.at[c], (across, lev))

    barrier = pltpu.get_barrier_semaphore()

    def greet(device):
        pl.semaphore_signal(barrier, inc=1, device_id=device, device_id_type=MESH)

    @pl.when(has_south)
    def _():
        greet((lat - 1, lev))

    @pl.when(has_north)
    def _():
        greet((lat + 1, lev))

    for s in range(1, n_lev):
        greet((lat, lax.rem(lev + s, n_lev)))
    greet((across, lev))
    beside = jnp.minimum(lat, 1) + jnp.minimum(n_lat - 1 - lat, 1)
    pl.semaphore_wait(barrier, n_lev + beside)

    @pl.when(has_south)
    def _():
        face.start()

    @pl.when(jnp.logical_not(has_north))
    def _():
        above[...] = jnp.zeros_like(above)
        north[...] = jnp.zeros_like(north)

    @pl.when(jnp.logical_not(has_south))
    def _():
        south[...] = jnp.zeros_like(south)

    def split(c, carry):
        row = lax.broadcasted_iota(jnp.int32, (unit, 2 * unit), 0)
        column = lax.broadcasted_iota(jnp.int32, (unit, 2 * unit), 1)
        whole = tracer_ref[c]
        for a, ref in enumerate((row0, row1)):
            pick = (column == 2 * row + a).astype(f32).astype(whole.dtype)
            ref[c] = jnp.dot(pick, whole, preferred_element_type=f32).astype(ref.dtype)

        @pl.when(has_north)
        def _():
            up(c).start()

        @pl.when(has_south)
        def _():
            down(c).start()

        return carry

    lax.fori_loop(0, chunks, split, 0)

    @pl.when(has_north)
    def _():
        face.wait_recv()

    def lon_change(q, cw):
        west = cw * jnp.where(cw > 0, pltpu.roll(q, 1, 1), q)
        return pltpu.roll(west, lon - 1, 1) - west

    def advect(c):
        @pl.when(has_south)
        def _():
            up(c).wait_recv()

        @pl.when(has_north)
        def _():
            down(c).wait_recv()

        def strip(s, carry):
            at = pl.ds(pl.multiple_of(s * STRIP, STRIP), STRIP)
            q0, q1 = row0[c, at, :].astype(f32), row1[c, at, :].astype(f32)
            cs0, cs1, cw0, cw1 = (faces_ref[f, at, :].astype(f32) for f in range(4))
            cn = above[at, :].astype(f32)
            low = cs0 * jnp.where(cs0 > 0, south[c, at, :].astype(f32), q0)
            mid = cs1 * jnp.where(cs1 > 0, q0, q1)
            high = cn * jnp.where(cn > 0, q1, north[c, at, :].astype(f32))
            new0 = (q0 - (mid - low) - lon_change(q0, cw0)).astype(advected.dtype)
            new1 = (q1 - (high - mid) - lon_change(q1, cw1)).astype(advected.dtype)
            for j in range(n_lev):
                advected[c, j, at, :block] = new0[:, j * block:(j + 1) * block]
                advected[c, j, at, block:] = new1[:, j * block:(j + 1) * block]
            return carry

        lax.fori_loop(0, unit // STRIP, strip, 0)
        for s in range(1, n_lev):
            exchange(c, s).start()
        own(c).start()

    def physics(c):
        for s in range(1, n_lev):
            exchanged(c, s).wait_recv()
        own(c).wait()

        def span(i, carry):
            lanes = pl.ds(pl.multiple_of(i * LANES, LANES), LANES)
            for g in range(n_lev):
                x_ref[g] = jnp.dot(arrived[c, g], placing_ref[:, lanes], preferred_element_type=f32)
            rain = rain_ref[:, lanes].astype(f32)

            def group(h, carry):
                t0 = h * GROUP
                sums = tuple(jnp.zeros((levels, LANES), f32) for _ in range(GROUP))
                for g in range(n_lev):
                    def level(e, sums):
                        m = matrix_ref[g * per + e, :, lanes].astype(f32)
                        return tuple(
                            total + m * x_ref[g, pl.ds((t0 + u) * per + e, 1), :]
                            for u, total in enumerate(sums)
                        )
                    sums = lax.fori_loop(0, per, level, sums, unroll=True)
                for u in range(GROUP):
                    t = c * UNIT + t0 + u
                    out = sums[u] * jnp.exp(-scav_ref[t] * rain)
                    washed_ref[t, :, lanes] = out.astype(washed_ref.dtype)
                return carry

            return lax.fori_loop(0, UNIT // GROUP, group, carry)

        lax.fori_loop(0, columns // LANES, span, 0)
        trade(c).start()

    advect(0)

    def step(c, carry):
        @pl.when(c < chunks - 1)
        def _():
            advect(c + 1)

        physics(c)
        return carry

    lax.fori_loop(0, chunks, step, 0)

    def finish(c, carry):
        @pl.when(has_north)
        def _():
            up(c).wait_send()

        @pl.when(has_south)
        def _():
            down(c).wait_send()

        for s in range(1, n_lev):
            exchange(c, s).wait_send()
        trade(c).wait()
        return carry

    lax.fori_loop(0, chunks, finish, 0)

    @pl.when(has_south)
    def _():
        face.wait_send()


def local(tracer_dyn, courant_lat, courant_lon, conv_matrix, conv_mask, column_order, rain, scav_rate, pair_flag):
    n_lat = lax.axis_size("lat")
    n_lev = lax.axis_size("lev")
    tracers, per, _, lon = tracer_dyn.shape
    levels, _, columns = conv_matrix.shape
    chunks, unit = tracers // UNIT, UNIT * per
    dtype = tracer_dyn.dtype

    faces = jnp.stack([courant_lat[:, 0], courant_lat[:, 1], courant_lon[:, 0], courant_lon[:, 1]])
    faces = jnp.tile(faces, (1, UNIT, 1))
    placing = (jnp.arange(columns, dtype=jnp.int32)[:, None] == column_order[None, :]).astype(dtype)
    keep = jnp.eye(levels, dtype=conv_matrix.dtype)[:, :, None]
    matrix = jnp.where(conv_mask[None, None, :] > 0, jnp.transpose(conv_matrix, (1, 0, 2)), keep)

    vmem = pl.BlockSpec(memory_space=pltpu.VMEM)
    whole = jax.ShapeDtypeStruct((tracers, levels, columns), dtype)
    dma = pltpu.SemaphoreType.DMA
    rows = pltpu.VMEM((chunks, unit, lon), dtype)
    spans = pltpu.VMEM((chunks, n_lev, unit, columns), dtype)
    washed, partner = pl.pallas_call(
        functools.partial(kernel, n_lat, n_lev),
        in_specs=[pl.BlockSpec(memory_space=pltpu.SMEM)] + [vmem] * 5,
        out_specs=[vmem, vmem],
        out_shape=[whole, whole],
        scratch_shapes=[
            rows, rows, rows, rows, pltpu.VMEM((unit, lon), dtype), spans, spans,
            pltpu.VMEM((n_lev, unit, LANES), jnp.float32),
            dma((chunks,)), dma((chunks,)), dma((chunks,)), dma((chunks,)), dma, dma,
            dma((chunks, n_lev)), dma((chunks, n_lev)), dma((chunks,)), dma((chunks,)), dma((chunks,)),
        ],
        compiler_params=pltpu.CompilerParams(
            collective_id=0, has_side_effects=True, vmem_limit_bytes=56 * 2**20),
        cost_estimate=pl.CostEstimate(
            flops=2 * tracers * levels * levels * columns,
            bytes_accessed=8 * tracers * levels * columns,
            transcendentals=tracers * levels * columns),
        name="substep",
    )(scav_rate, tracer_dyn.reshape(chunks, 2 * unit, lon), faces, placing, matrix, rain)

    pair = lax.axis_index("lat") % (n_lat // 2) * n_lev + lax.axis_index("lev")
    return jnp.where(pair_flag[pair] > 0, partner, washed)


def solution(mesh):
    placed = (
        P(None, "lev", "lat", None),
        P("lev", "lat", None),
        P("lev", "lat", None),
        P(None, None, ("lat", "lev")),
        P(("lat", "lev")),
        P(("lat", "lev")),
        P(None, ("lat", "lev")),
        P(),
        P(),
    )
    return jax.shard_map(
        local, mesh=mesh, in_specs=placed, out_specs=P(None, None, ("lat", "lev")), check_vma=False
    )
```

```python
import functools

import jax
import jax.numpy as jnp
from jax import lax
from jax.experimental import pallas as pl
from jax.experimental.pallas import tpu as pltpu
from jax.sharding import PartitionSpec as P

UNIT = 8
STRIP = 16
LANES = 128
GROUP = 4
AHEAD = 2
MESH = pl.DeviceIdType.MESH


def kernel(
    n_lat, n_lev, scav_ref, tracer_ref, faces_ref, placing_ref, matrix_ref, rain_ref,
    washed_ref, partner_ref,
    row0, row1, south, north, above, advected, arrived, x_ref,
    up_send, up_recv, down_send, down_recv, face_send, face_recv,
    lev_send, lev_recv, own_sem, trade_send, trade_recv,
):
    f32 = jnp.float32
    chunks, unit, lon = row0.shape
    tracers, levels, columns = washed_ref.shape
    block = lon // n_lev
    per = levels // n_lev
    lat, lev = lax.axis_index("lat"), lax.axis_index("lev")
    has_south, has_north = lat > 0, lat < n_lat - 1
    across = lax.rem(lat + n_lat // 2, n_lat)

    def remote(src, dst, send, recv, device):
        return pltpu.make_async_remote_copy(
            src_ref=src, dst_ref=dst, send_sem=send, recv_sem=recv,
            device_id=device, device_id_type=MESH)

    def up(c):
        return remote(row1.at[c], south.at[c], up_send.at[c], up_recv.at[c], (lat + 1, lev))

    def down(c):
        return remote(row0.at[c], north.at[c], down_send.at[c], down_recv.at[c], (lat - 1, lev))

    face = remote(faces_ref.at[0], above, face_send, face_recv, (lat - 1, lev))

    def exchange(c, s):
        to = lax.rem(lev + s, n_lev)
        return remote(advected.at[c, to], arrived.at[c, lev],
                      lev_send.at[c, s], lev_recv.at[c, s], (lat, to))

    def exchanged(c, s):
        source = lax.rem(lev + n_lev - s, n_lev)
        return remote(advected.at[c, source], arrived.at[c, source],
                      lev_send.at[c, s], lev_recv.at[c, s], (lat, source))

    def own(c):
        return pltpu.make_async_copy(advected.at[c, lev], arrived.at[c, lev], own_sem.at[c])

    def trade(c):
        part = pl.ds(c * UNIT, UNIT)
        return remote(washed_ref.at[part], partner_ref.at[part],
                      trade_send.at[c], trade_recv.at[c], (across, lev))

    barrier = pltpu.get_barrier_semaphore()

    def greet(device):
        pl.semaphore_signal(barrier, inc=1, device_id=device, device_id_type=MESH)

    @pl.when(has_south)
    def _():
        greet((lat - 1, lev))

    @pl.when(has_north)
    def _():
        greet((lat + 1, lev))

    for s in range(1, n_lev):
        greet((lat, lax.rem(lev + s, n_lev)))
    greet((across, lev))
    beside = jnp.minimum(lat, 1) + jnp.minimum(n_lat - 1 - lat, 1)
    pl.semaphore_wait(barrier, n_lev + beside)

    @pl.when(has_south)
    def _():
        face.start()

    @pl.when(jnp.logical_not(has_north))
    def _():
        above[...] = jnp.zeros_like(above)
        north[...] = jnp.zeros_like(north)

    @pl.when(jnp.logical_not(has_south))
    def _():
        south[...] = jnp.zeros_like(south)

    def halo(c):
        @pl.when(has_north)
        def _():
            up(c).start()

        @pl.when(has_south)
        def _():
            down(c).start()

    def split(c, carry):
        row = lax.broadcasted_iota(jnp.int32, (unit, 2 * unit), 0)
        column = lax.broadcasted_iota(jnp.int32, (unit, 2 * unit), 1)
        whole = tracer_ref[c]
        for a, ref in enumerate((row0, row1)):
            pick = (column == 2 * row + a).astype(f32).astype(whole.dtype)
            ref[c] = jnp.dot(pick, whole, preferred_element_type=f32).astype(ref.dtype)

        @pl.when(c < AHEAD)
        def _():
            halo(c)

        return carry

    lax.fori_loop(0, chunks, split, 0)

    @pl.when(has_north)
    def _():
        face.wait_recv()

    def lon_change(q, cw):
        west = cw * jnp.where(cw > 0, pltpu.roll(q, 1, 1), q)
        return pltpu.roll(west, lon - 1, 1) - west

    def advect(c):
        @pl.when(has_south)
        def _():
            up(c).wait_recv()

        @pl.when(has_north)
        def _():
            down(c).wait_recv()

        for later in range(AHEAD):
            following = AHEAD * (c + 1) + later

            @pl.when(following < chunks)
            def _():
                halo(following)

        def strip(s, carry):
            at = pl.ds(pl.multiple_of(s * STRIP, STRIP), STRIP)
            q0, q1 = row0[c, at, :].astype(f32), row1[c, at, :].astype(f32)
            cs0, cs1, cw0, cw1 = (faces_ref[f, at, :].astype(f32) for f in range(4))
            cn = above[at, :].astype(f32)
            low = cs0 * jnp.where(cs0 > 0, south[c, at, :].astype(f32), q0)
            mid = cs1 * jnp.where(cs1 > 0, q0, q1)
            high = cn * jnp.where(cn > 0, q1, north[c, at, :].astype(f32))
            new0 = (q0 - (mid - low) - lon_change(q0, cw0)).astype(advected.dtype)
            new1 = (q1 - (high - mid) - lon_change(q1, cw1)).astype(advected.dtype)
            for j in range(n_lev):
                advected[c, j, at, :block] = new0[:, j * block:(j + 1) * block]
                advected[c, j, at, block:] = new1[:, j * block:(j + 1) * block]
            return carry

        lax.fori_loop(0, unit // STRIP, strip, 0)
        for s in range(1, n_lev):
            exchange(c, s).start()
        own(c).start()

    def physics(c):
        for s in range(1, n_lev):
            exchanged(c, s).wait_recv()
        own(c).wait()

        def span(i, carry):
            lanes = pl.ds(pl.multiple_of(i * LANES, LANES), LANES)
            for g in range(n_lev):
                x_ref[g] = jnp.dot(arrived[c, g], placing_ref[:, lanes], preferred_element_type=f32)
            rain = rain_ref[:, lanes].astype(f32)

            def group(h, carry):
                t0 = h * GROUP
                sums = tuple(jnp.zeros((levels, LANES), f32) for _ in range(GROUP))
                for g in range(n_lev):
                    def level(e, sums):
                        m = matrix_ref[g * per + e, :, lanes].astype(f32)
                        return tuple(
                            total + m * x_ref[g, pl.ds((t0 + u) * per + e, 1), :]
                            for u, total in enumerate(sums)
                        )
                    sums = lax.fori_loop(0, per, level, sums, unroll=True)
                for u in range(GROUP):
                    t = c * UNIT + t0 + u
                    out = sums[u] * jnp.exp(-scav_ref[t] * rain)
                    washed_ref[t, :, lanes] = out.astype(washed_ref.dtype)
                return carry

            return lax.fori_loop(0, UNIT // GROUP, group, carry)

        lax.fori_loop(0, columns // LANES, span, 0)
        trade(c).start()

    advect(0)

    def step(c, carry):
        @pl.when(c < chunks - 1)
        def _():
            advect(c + 1)

        physics(c)
        return carry

    lax.fori_loop(0, chunks, step, 0)

    def finish(c, carry):
        @pl.when(has_north)
        def _():
            up(c).wait_send()

        @pl.when(has_south)
        def _():
            down(c).wait_send()

        for s in range(1, n_lev):
            exchange(c, s).wait_send()
        trade(c).wait()
        return carry

    lax.fori_loop(0, chunks, finish, 0)

    @pl.when(has_south)
    def _():
        face.wait_send()


def local(tracer_dyn, courant_lat, courant_lon, conv_matrix, conv_mask, column_order, rain, scav_rate, pair_flag):
    n_lat = lax.axis_size("lat")
    n_lev = lax.axis_size("lev")
    tracers, per, _, lon = tracer_dyn.shape
    levels, _, columns = conv_matrix.shape
    chunks, unit = tracers // UNIT, UNIT * per
    dtype = tracer_dyn.dtype

    faces = jnp.stack([courant_lat[:, 0], courant_lat[:, 1], courant_lon[:, 0], courant_lon[:, 1]])
    faces = jnp.tile(faces, (1, UNIT, 1))
    placing = (jnp.arange(columns, dtype=jnp.int32)[:, None] == column_order[None, :]).astype(dtype)
    keep = jnp.eye(levels, dtype=conv_matrix.dtype)[:, :, None]
    matrix = jnp.where(conv_mask[None, None, :] > 0, jnp.transpose(conv_matrix, (1, 0, 2)), keep)

    vmem = pl.BlockSpec(memory_space=pltpu.VMEM)
    whole = jax.ShapeDtypeStruct((tracers, levels, columns), dtype)
    dma = pltpu.SemaphoreType.DMA
    rows = pltpu.VMEM((chunks, unit, lon), dtype)
    spans = pltpu.VMEM((chunks, n_lev, unit, columns), dtype)
    washed, partner = pl.pallas_call(
        functools.partial(kernel, n_lat, n_lev),
        in_specs=[pl.BlockSpec(memory_space=pltpu.SMEM)] + [vmem] * 5,
        out_specs=[vmem, vmem],
        out_shape=[whole, whole],
        scratch_shapes=[
            rows, rows, rows, rows, pltpu.VMEM((unit, lon), dtype), spans, spans,
            pltpu.VMEM((n_lev, unit, LANES), jnp.float32),
            dma((chunks,)), dma((chunks,)), dma((chunks,)), dma((chunks,)), dma, dma,
            dma((chunks, n_lev)), dma((chunks, n_lev)), dma((chunks,)), dma((chunks,)), dma((chunks,)),
        ],
        compiler_params=pltpu.CompilerParams(
            collective_id=0, has_side_effects=True, vmem_limit_bytes=56 * 2**20),
        cost_estimate=pl.CostEstimate(
            flops=2 * tracers * levels * levels * columns,
            bytes_accessed=8 * tracers * levels * columns,
            transcendentals=tracers * levels * columns),
        name="substep",
    )(scav_rate, tracer_dyn.reshape(chunks, 2 * unit, lon), faces, placing, matrix, rain)

    pair = lax.axis_index("lat") % (n_lat // 2) * n_lev + lax.axis_index("lev")
    return jnp.where(pair_flag[pair] > 0, partner, washed)


def solution(mesh):
    placed = (
        P(None, "lev", "lat", None),
        P("lev", "lat", None),
        P("lev", "lat", None),
        P(None, None, ("lat", "lev")),
        P(("lat", "lev")),
        P(("lat", "lev")),
        P(None, ("lat", "lev")),
        P(),
        P(),
    )
    return jax.shard_map(
        local, mesh=mesh, in_specs=placed, out_specs=P(None, None, ("lat", "lev")), check_vma=False
    )
```

```python
import functools

import jax
import jax.numpy as jnp
from jax import lax
from jax.experimental import pallas as pl
from jax.experimental.pallas import tpu as pltpu
from jax.sharding import PartitionSpec as P

UNIT = 8
STRIP = 16
LANES = 128
GROUP = 4
AHEAD = 2
MESH = pl.DeviceIdType.MESH


def kernel(
    n_lat, n_lev, scav_ref, tracer_ref, faces_ref, placing_ref, matrix_ref, rain_ref,
    washed_ref, partner_ref,
    row0, row1, south, north, hop, above, advected, arrived, x_ref,
    up_send, up_recv, down_send, down_recv, face_send, face_recv,
    lev_send, lev_recv, own_sem, trade_send, trade_recv, hop_send, hop_recv, on_send,
):
    f32 = jnp.float32
    chunks, unit, lon = row0.shape
    tracers, levels, columns = washed_ref.shape
    block = lon // n_lev
    per = levels // n_lev
    lat, lev = lax.axis_index("lat"), lax.axis_index("lev")
    has_south, has_north = lat > 0, lat < n_lat - 1
    across = lax.rem(lat + n_lat // 2, n_lat)

    def remote(src, dst, send, recv, device):
        return pltpu.make_async_remote_copy(
            src_ref=src, dst_ref=dst, send_sem=send, recv_sem=recv,
            device_id=device, device_id_type=MESH)

    def up(c):
        return remote(row1.at[c], south.at[c], up_send.at[c], up_recv.at[c], (lat + 1, lev))

    def down(c):
        return remote(row0.at[c], north.at[c], down_send.at[c], down_recv.at[c], (lat - 1, lev))

    half = n_lat // 2

    def hop_up(c):
        return remote(row1.at[c], hop.at[c], hop_send.at[c], hop_recv.at[c], (lat + 2, lev))

    def hop_down(c):
        return remote(row0.at[c], hop.at[c], hop_send.at[c], hop_recv.at[c], (lat - 2, lev))

    def on_up(c):
        return remote(hop.at[c], south.at[c], on_send.at[c], up_recv.at[c], (lat - 1, lev))

    def on_down(c):
        return remote(hop.at[c], north.at[c], on_send.at[c], down_recv.at[c], (lat + 1, lev))

    def hops(c):
        return jnp.logical_and(c >= 3, lax.rem(c, 2) == 1)

    def forward(c):
        for where, copy, passed in ((half + 1, hop_up, on_up), (half - 2, hop_down, on_down)):
            @pl.when(jnp.logical_and(hops(c), lat == where))
            def _():
                copy(c).wait_recv()
                passed(c).start()

    def direct(c, side):
        return jnp.logical_not(jnp.logical_and(hops(c), lat == side))

    face = remote(faces_ref.at[0], above, face_send, face_recv, (lat - 1, lev))

    def exchange(c, s):
        to = lax.rem(lev + s, n_lev)
        return remote(advected.at[c, to], arrived.at[c, lev],
                      lev_send.at[c, s], lev_recv.at[c, s], (lat, to))

    def exchanged(c, s):
        source = lax.rem(lev + n_lev - s, n_lev)
        return remote(advected.at[c, source], arrived.at[c, source],
                      lev_send.at[c, s], lev_recv.at[c, s], (lat, source))

    def own(c):
        return pltpu.make_async_copy(advected.at[c, lev], arrived.at[c, lev], own_sem.at[c])

    def trade(c):
        part = pl.ds(c * UNIT, UNIT)
        return remote(washed_ref.at[part], partner_ref.at[part],
                      trade_send.at[c], trade_recv.at[c], (across, lev))

    barrier = pltpu.get_barrier_semaphore()

    def greet(device):
        pl.semaphore_signal(barrier, inc=1, device_id=device, device_id_type=MESH)

    @pl.when(has_south)
    def _():
        greet((lat - 1, lev))

    @pl.when(has_north)
    def _():
        greet((lat + 1, lev))

    for s in range(1, n_lev):
        greet((lat, lax.rem(lev + s, n_lev)))
    greet((across, lev))
    for here, there in ((half - 1, 2), (half + 1, -2), (half, -2), (half - 2, 2)):
        @pl.when(lat == here)
        def _():
            greet((lat + there, lev))

    middle = jnp.where(jnp.logical_and(lat >= half - 2, lat <= half + 1), 1, 0)
    beside = jnp.minimum(lat, 1) + jnp.minimum(n_lat - 1 - lat, 1) + middle
    pl.semaphore_wait(barrier, n_lev + beside)

    @pl.when(has_south)
    def _():
        face.start()

    @pl.when(jnp.logical_not(has_north))
    def _():
        above[...] = jnp.zeros_like(above)
        north[...] = jnp.zeros_like(north)

    @pl.when(jnp.logical_not(has_south))
    def _():
        south[...] = jnp.zeros_like(south)

    def halo(c):
        @pl.when(jnp.logical_and(has_north, direct(c, half - 1)))
        def _():
            up(c).start()

        @pl.when(jnp.logical_and(has_south, direct(c, half)))
        def _():
            down(c).start()

        @pl.when(jnp.logical_and(hops(c), lat == half - 1))
        def _():
            hop_up(c).start()

        @pl.when(jnp.logical_and(hops(c), lat == half))
        def _():
            hop_down(c).start()

    def split(c, carry):
        row = lax.broadcasted_iota(jnp.int32, (unit, 2 * unit), 0)
        column = lax.broadcasted_iota(jnp.int32, (unit, 2 * unit), 1)
        whole = tracer_ref[c]
        for a, ref in enumerate((row0, row1)):
            pick = (column == 2 * row + a).astype(f32).astype(whole.dtype)
            ref[c] = jnp.dot(pick, whole, preferred_element_type=f32).astype(ref.dtype)

        @pl.when(c < AHEAD)
        def _():
            halo(c)

        return carry

    lax.fori_loop(0, chunks, split, 0)

    @pl.when(has_north)
    def _():
        face.wait_recv()

    def lon_change(q, cw):
        west = cw * jnp.where(cw > 0, pltpu.roll(q, 1, 1), q)
        return pltpu.roll(west, lon - 1, 1) - west

    def advect(c):
        @pl.when(has_south)
        def _():
            up(c).wait_recv()

        @pl.when(has_north)
        def _():
            down(c).wait_recv()

        for later in range(AHEAD):
            following = AHEAD * (c + 1) + later

            @pl.when(following < chunks)
            def _():
                halo(following)

        def strip(s, carry):
            at = pl.ds(pl.multiple_of(s * STRIP, STRIP), STRIP)
            q0, q1 = row0[c, at, :].astype(f32), row1[c, at, :].astype(f32)
            cs0, cs1, cw0, cw1 = (faces_ref[f, at, :].astype(f32) for f in range(4))
            cn = above[at, :].astype(f32)
            low = cs0 * jnp.where(cs0 > 0, south[c, at, :].astype(f32), q0)
            mid = cs1 * jnp.where(cs1 > 0, q0, q1)
            high = cn * jnp.where(cn > 0, q1, north[c, at, :].astype(f32))
            new0 = (q0 - (mid - low) - lon_change(q0, cw0)).astype(advected.dtype)
            new1 = (q1 - (high - mid) - lon_change(q1, cw1)).astype(advected.dtype)
            for j in range(n_lev):
                advected[c, j, at, :block] = new0[:, j * block:(j + 1) * block]
                advected[c, j, at, block:] = new1[:, j * block:(j + 1) * block]
            return carry

        lax.fori_loop(0, unit // STRIP, strip, 0)
        for s in range(1, n_lev):
            exchange(c, s).start()
        own(c).start()

    def physics(c):
        for s in range(1, n_lev):
            exchanged(c, s).wait_recv()
        own(c).wait()

        def span(i, carry):
            lanes = pl.ds(pl.multiple_of(i * LANES, LANES), LANES)
            for g in range(n_lev):
                x_ref[g] = jnp.dot(arrived[c, g], placing_ref[:, lanes], preferred_element_type=f32)
            rain = rain_ref[:, lanes].astype(f32)

            def group(h, carry):
                t0 = h * GROUP
                sums = tuple(jnp.zeros((levels, LANES), f32) for _ in range(GROUP))
                for g in range(n_lev):
                    def level(e, sums):
                        m = matrix_ref[g * per + e, :, lanes].astype(f32)
                        return tuple(
                            total + m * x_ref[g, pl.ds((t0 + u) * per + e, 1), :]
                            for u, total in enumerate(sums)
                        )
                    sums = lax.fori_loop(0, per, level, sums, unroll=True)
                for u in range(GROUP):
                    t = c * UNIT + t0 + u
                    out = sums[u] * jnp.exp(-scav_ref[t] * rain)
                    washed_ref[t, :, lanes] = out.astype(washed_ref.dtype)
                return carry

            return lax.fori_loop(0, UNIT // GROUP, group, carry)

        lax.fori_loop(0, columns // LANES, span, 0)
        trade(c).start()

    advect(0)

    def step(c, carry):
        @pl.when(c < chunks - 1)
        def _():
            advect(c + 1)

        @pl.when(c < chunks - 2)
        def _():
            forward(c + 2)

        physics(c)
        return carry

    lax.fori_loop(0, chunks, step, 0)

    def finish(c, carry):
        @pl.when(jnp.logical_and(has_north, direct(c, half - 1)))
        def _():
            up(c).wait_send()

        @pl.when(jnp.logical_and(has_south, direct(c, half)))
        def _():
            down(c).wait_send()

        for where, copy in ((half - 1, hop_up), (half, hop_down), (half + 1, on_up), (half - 2, on_down)):
            @pl.when(jnp.logical_and(hops(c), lat == where))
            def _():
                copy(c).wait_send()

        for s in range(1, n_lev):
            exchange(c, s).wait_send()
        trade(c).wait()
        return carry

    lax.fori_loop(0, chunks, finish, 0)

    @pl.when(has_south)
    def _():
        face.wait_send()


def local(tracer_dyn, courant_lat, courant_lon, conv_matrix, conv_mask, column_order, rain, scav_rate, pair_flag):
    n_lat = lax.axis_size("lat")
    n_lev = lax.axis_size("lev")
    tracers, per, _, lon = tracer_dyn.shape
    levels, _, columns = conv_matrix.shape
    chunks, unit = tracers // UNIT, UNIT * per
    dtype = tracer_dyn.dtype

    faces = jnp.stack([courant_lat[:, 0], courant_lat[:, 1], courant_lon[:, 0], courant_lon[:, 1]])
    faces = jnp.tile(faces, (1, UNIT, 1))
    placing = (jnp.arange(columns, dtype=jnp.int32)[:, None] == column_order[None, :]).astype(dtype)
    keep = jnp.eye(levels, dtype=conv_matrix.dtype)[:, :, None]
    matrix = jnp.where(conv_mask[None, None, :] > 0, jnp.transpose(conv_matrix, (1, 0, 2)), keep)

    vmem = pl.BlockSpec(memory_space=pltpu.VMEM)
    whole = jax.ShapeDtypeStruct((tracers, levels, columns), dtype)
    dma = pltpu.SemaphoreType.DMA
    rows = pltpu.VMEM((chunks, unit, lon), dtype)
    spans = pltpu.VMEM((chunks, n_lev, unit, columns), dtype)
    washed, partner = pl.pallas_call(
        functools.partial(kernel, n_lat, n_lev),
        in_specs=[pl.BlockSpec(memory_space=pltpu.SMEM)] + [vmem] * 5,
        out_specs=[vmem, vmem],
        out_shape=[whole, whole],
        scratch_shapes=[
            rows, rows, rows, rows, rows, pltpu.VMEM((unit, lon), dtype), spans, spans,
            pltpu.VMEM((n_lev, unit, LANES), jnp.float32),
            dma((chunks,)), dma((chunks,)), dma((chunks,)), dma((chunks,)), dma, dma,
            dma((chunks, n_lev)), dma((chunks, n_lev)), dma((chunks,)), dma((chunks,)), dma((chunks,)),
            dma((chunks,)), dma((chunks,)), dma((chunks,)),
        ],
        compiler_params=pltpu.CompilerParams(
            collective_id=0, has_side_effects=True, vmem_limit_bytes=56 * 2**20),
        cost_estimate=pl.CostEstimate(
            flops=2 * tracers * levels * levels * columns,
            bytes_accessed=8 * tracers * levels * columns,
            transcendentals=tracers * levels * columns),
        name="substep",
    )(scav_rate, tracer_dyn.reshape(chunks, 2 * unit, lon), faces, placing, matrix, rain)

    pair = lax.axis_index("lat") % (n_lat // 2) * n_lev + lax.axis_index("lev")
    return jnp.where(pair_flag[pair] > 0, partner, washed)


def solution(mesh):
    placed = (
        P(None, "lev", "lat", None),
        P("lev", "lat", None),
        P("lev", "lat", None),
        P(None, None, ("lat", "lev")),
        P(("lat", "lev")),
        P(("lat", "lev")),
        P(None, ("lat", "lev")),
        P(),
        P(),
    )
    return jax.shard_map(
        local, mesh=mesh, in_specs=placed, out_specs=P(None, None, ("lat", "lev")), check_vma=False
    )
```
